256 devices in a mesh: dom: 128 (over x, z, y), slab: 2 (over core).
Axes of the slice: x: 4, y: 4, z: 8, core: 2. Of those that a mesh axis runs over, the one named last changes fastest.
Arguments:
- positions: float32 [3, 8388608], P(None, ('dom', 'slab')), may hold values from -6 to 6
- velocities: float32 [3, 8388608], P(None, ('dom', 'slab')), may hold values from -6 to 6
- destination: int32 [8388608], P(('dom', 'slab')), may hold values from 0 to 4, as said below
- live_count: int32 [256], P(('dom', 'slab')), may hold values from 24576 to 32768
- ghost_list: int32 [256, 4, 32], P(('dom', 'slab')), may hold values from 0 to 271
- pair_blocks: int32 [256, 512, 2], P(('dom', 'slab')), may hold values from 0 to 671, as said below
- pair_count: int32 [256], P(('dom', 'slab')), may hold values from 128 to 512, as said below
Outputs:
- new_positions: float32 [3, 8912896], P(None, ('dom', 'slab'))
- new_velocities: float32 [3, 8912896], P(None, ('dom', 'slab'))
The draws below stay inside these ranges and needn't reach their ends.
Inputs may be any that keep to these rules, and one draw needn't show every extreme that they name: `destination`: among the 32768 slots of one device at most 512 carry the same nonzero code, and exactly 512 carry each nonzero code on some devices. `pair_blocks`: the first entry of a pair is an own block; the second indexes the pool: own blocks, then the slab partner's blocks, then ghost blocks by direction and position. `pair_count`: at most 512, reached on some devices.
All inputs are finite; a program needn't handle non-finite values.
Results may differ from the reference program's by a relative error of at most 0.0003.
Values sent between devices are 32-bit elements; how exact they have to be, the bound alone decides.
A program may use at most 64 MiB of HBM per device.

```python
import math
import jax
import jax.numpy as jnp
from jax import lax

P_DEV = 32768
NPAIR = 512
BLOCK = 128
MOVE = 512
GHOST = 32
NDEV = 256
PARTS_SIZE = 8388608
BUF = 34816
NBLK = 272
POOL = 672
HOP = 32
N_DOM = 128
N_SLAB = 2


def draw_destination(key, part):
    key = jax.random.fold_in(key, 5)
    keys = jax.random.split(key, 3)
    counts = jax.random.randint(keys[0], (NDEV, 4), MOVE // 8, MOVE // 2 + 1)
    heavy = jax.random.permutation(keys[1], NDEV) < max(NDEV // 8, 1)
    counts = jnp.where(heavy[:, None], MOVE, counts).astype(jnp.int32)
    totals = jnp.cumsum(counts, axis=1).astype(jnp.int32)
    rank = jnp.arange(P_DEV, dtype=jnp.int32)[None, :]
    passed = (rank >= totals[:, 0:1]).astype(jnp.int32) + (rank >= totals[:, 1:2]).astype(jnp.int32) + (rank >= totals[:, 2:3]).astype(jnp.int32)
    code_at_rank = jnp.where(rank < totals[:, 3:4], 1 + passed, 0).astype(jnp.int32)
    orders = jax.vmap(lambda one_key: jax.random.permutation(one_key, P_DEV))(jax.random.split(keys[2], NDEV)).astype(jnp.int32)
    rows_index = jnp.arange(NDEV, dtype=jnp.int32)[:, None]
    codes = jnp.zeros((NDEV, P_DEV), jnp.int32).at[rows_index, orders].set(code_at_rank)
    return codes.reshape(NDEV * P_DEV).astype(jnp.int32)


def draw_pair_blocks(key, part):
    key = jax.random.fold_in(key, 11)
    keys = jax.random.split(key, 5)
    near_pick = jax.random.randint(keys[0], (NDEV, NPAIR), 0, NBLK)
    source_kind = jax.random.randint(keys[1], (NDEV, NPAIR), 0, 3)
    own_pick = jax.random.randint(keys[2], (NDEV, NPAIR), 0, NBLK)
    partner_pick = NBLK + jax.random.randint(keys[3], (NDEV, NPAIR), 0, NBLK)
    ghost_pick = 2 * NBLK + jax.random.randint(keys[4], (NDEV, NPAIR), 0, 4 * GHOST)
    far_pick = jnp.where(source_kind == 0, own_pick, jnp.where(source_kind == 1, partner_pick, ghost_pick))
    return jnp.stack([near_pick, far_pick], axis=-1).astype(jnp.int32)


def draw_pair_count(key, part):
    key = jax.random.fold_in(key, 23)
    keys = jax.random.split(key, 2)
    base_count = jax.random.randint(keys[0], (NDEV,), NPAIR // 4, NPAIR // 2 + 1)
    shuffled = jax.random.permutation(keys[1], NDEV)
    busiest = shuffled < max(NDEV // 16, 1)
    return jnp.where(busiest, NPAIR, base_count).astype(jnp.int32)


def set_ends(entries, own_key, smallest, high):
    extent = entries.shape
    index_at = [jax.random.randint(jax.random.fold_in(own_key, axis), (), 0, extent[axis]) for axis in range(len(extent))]
    entries = entries.at[tuple(index_at)].set(smallest)
    longest = extent.index(max(extent))
    index_at[longest] = (index_at[longest] + 1) % extent[longest]
    return entries.at[tuple(index_at)].set(high)


def steps_of(rng, shape, shards, low, top_value):
    level = 1.0
    for dim, shards_of in shards:
        steps = jax.random.uniform(jax.random.fold_in(jax.random.fold_in(rng, 6), dim), (shards_of,), jnp.float32, low / len(shards), top_value / len(shards))
        level = level * jnp.repeat(jnp.exp(steps), shape[dim] // shards_of).reshape((-1,) + (1,) * (len(shape) - 1 - dim))
    return level


def bell_draw(stream_key, dims, deviation, reach, cuts=(), kind=jnp.bfloat16):
    array = jax.random.normal(stream_key, dims, jnp.float32) * deviation
    if len(cuts) > 0:
        array = steps_of(stream_key, dims, cuts, -0.22, 0.18) * array
    return jnp.clip(array, min=-reach, max=reach).astype(kind)


def setup_inputs(seed: int = 0) -> dict:
    streams_of = jax.random.split(jax.random.key(seed), 8)
    positions = bell_draw(streams_of[0], (3, PARTS_SIZE), 1.0, 6.0, ((1, 256),), jnp.float32)
    velocities = bell_draw(streams_of[1], (3, PARTS_SIZE), 1.0, 6.0, ((1, 256),), jnp.float32)
    destination = draw_destination(jax.random.fold_in(streams_of[7], 71), 0)
    live_count = set_ends(jax.random.randint(streams_of[3], (NDEV,), 3 * P_DEV // 4, P_DEV + 1), jax.random.fold_in(streams_of[3], 1), 3 * P_DEV // 4, P_DEV).astype(jnp.int32)
    ghost_list = set_ends(jax.random.randint(streams_of[4], (NDEV, 4, GHOST), 0, NBLK), jax.random.fold_in(streams_of[4], 1), 0, NBLK - 1).astype(jnp.int32)
    pair_blocks = draw_pair_blocks(jax.random.fold_in(streams_of[7], 71), 0)
    pair_count = draw_pair_count(jax.random.fold_in(streams_of[7], 71), 0)
    return {"positions": positions, "velocities": velocities, "destination": destination, "live_count": live_count, "ghost_list": ghost_list, "pair_blocks": pair_blocks, "pair_count": pair_count}


soft_sq = 0.05
cutoff_sq = 9.0
screen_sq = 0.5
step_size = 0.25

def pair_forces(near_blocks, far_blocks, active):
    spacing = far_blocks[:3, :, None, :] - near_blocks[:3, :, :, None]
    sq_dist = spacing[0] * spacing[0] + spacing[1] * spacing[1] + spacing[2] * spacing[2]
    tapering = jnp.maximum(1.0 - sq_dist / cutoff_sq, 0.0)
    inv_root = lax.rsqrt(sq_dist + soft_sq)
    strength = inv_root * inv_root * inv_root * jnp.exp(-sq_dist / (4.0 * screen_sq)) * tapering * tapering
    strength = strength * near_blocks[3][:, :, None] * far_blocks[3][:, None, :] * active[:, None, None]
    weighted = strength[None] * spacing
    return (lax.optimization_barrier(jnp.sum(weighted, axis=3)), -lax.optimization_barrier(jnp.sum(weighted, axis=2)))

def migration_slots(codes, live_total, stay_len, move_cap, buffer_len):
    n_rows = codes.shape[0]
    position = jnp.arange(n_rows, dtype=jnp.int32)
    sort_key = jnp.where(position < live_total, codes, 5).astype(jnp.int32)
    sort_order = jnp.argsort(sort_key, stable=True).astype(jnp.int32)
    sorted_key = sort_key[sort_order]
    starts = jnp.searchsorted(sorted_key, jnp.arange(7, dtype=jnp.int32), side='left').astype(jnp.int32)
    rank_in = position - starts[sorted_key]
    moved_slot = stay_len + (sorted_key - 1) * move_cap + rank_in
    slot_sorted = jnp.where(sorted_key == 0, sort_order, jnp.where(sorted_key < 5, moved_slot, buffer_len)).astype(jnp.int32)
    slot_index = jnp.zeros((n_rows,), jnp.int32).at[sort_order].set(slot_sorted)
    return (slot_index, (starts[2:6] - starts[1:5]).astype(jnp.int32))

def reference(positions, velocities, destination, live_count, ghost_list, pair_blocks, pair_count):
    n_devices = N_DOM * N_SLAB
    drifted = positions + step_size * velocities
    payload = jnp.concatenate([drifted, velocities, jnp.ones((1, positions.shape[1]), positions.dtype)], axis=0)
    payload = payload.reshape(7, n_devices, P_DEV).transpose(1, 0, 2)
    codes = destination.reshape(n_devices, P_DEV)
    slots = jax.vmap(lambda code_row, live_total: migration_slots(code_row, live_total, P_DEV, MOVE, BUF)[0])(codes, live_count)

    def place(slot_index, rows):
        return jnp.zeros((7, BUF), rows.dtype).at[:, slot_index].set(rows, mode='drop')
    sectioned = jax.vmap(place)(slots, payload)
    offsets = (1, -1, HOP, -HOP)
    devices = jnp.arange(n_devices, dtype=jnp.int32)
    domains = devices // N_SLAB
    slabs = devices % N_SLAB
    pieces = [sectioned[:, :, :P_DEV]]
    for direction in range(4):
        source = (domains - offsets[direction]) % N_DOM * N_SLAB + slabs
        lower = P_DEV + direction * MOVE
        pieces.append(sectioned[:, :, lower:lower + MOVE][source])
    incoming = jnp.concatenate(pieces, axis=2)
    near_all = jnp.concatenate([incoming[:, :3], incoming[:, 6:7]], axis=1).reshape(n_devices, 4, NBLK, BLOCK)
    listed = jnp.arange(NPAIR, dtype=jnp.int32)

    def device_forces(device):
        domain = device // N_SLAB
        slab_index = device % N_SLAB
        own_blocks = near_all[device]
        parts_list = [own_blocks, near_all[jnp.bitwise_xor(device, 1)]]
        for direction in range(4):
            source = (domain - offsets[direction]) % N_DOM * N_SLAB + slab_index
            parts_list.append(jnp.take(near_all[source], ghost_list[source, direction], axis=1))
        pool_blocks = jnp.concatenate(parts_list, axis=1)
        active = (listed < pair_count[device]).astype(positions.dtype)

        def group_step(carry, group):
            force_acc, react_acc = carry
            near_pick, far_pick, live_pairs = group
            on_near, on_far = pair_forces(jnp.take(own_blocks, near_pick, axis=1), jnp.take(pool_blocks, far_pick, axis=1), live_pairs)
            return ((force_acc.at[:, near_pick].add(on_near), react_acc.at[:, far_pick].add(on_far)), None)
        groups = (pair_blocks[device, :, 0].reshape(-1, 16), pair_blocks[device, :, 1].reshape(-1, 16), active.reshape(-1, 16))
        start_carry = (jnp.zeros((3, NBLK, BLOCK), positions.dtype), jnp.zeros((3, POOL, BLOCK), positions.dtype))
        result, unused = lax.scan(group_step, start_carry, groups)
        return result
    force_near, reaction = lax.map(device_forces, devices)
    total_force = force_near + reaction[:, :, :NBLK] + reaction[:, :, NBLK:2 * NBLK][jnp.bitwise_xor(devices, 1)]
    for direction in range(4):
        source = (domains + offsets[direction]) % N_DOM * N_SLAB + slabs
        start_block = 2 * NBLK + direction * GHOST
        back = reaction[:, :, start_block:start_block + GHOST][source]
        total_force = jax.vmap(lambda acc, picks, extra: acc.at[:, picks].add(extra))(total_force, ghost_list[:, direction], back)
    kick = step_size / math.sqrt(BLOCK)
    new_positions = incoming[:, :3].transpose(1, 0, 2).reshape(3, n_devices * BUF)
    new_velocities = (incoming[:, 3:6] + kick * total_force.reshape(n_devices, 3, BUF)).transpose(1, 0, 2).reshape(3, n_devices * BUF)
    return (new_positions, new_velocities)
```

```python
import functools
import math

import jax
import jax.numpy as jnp
from jax import lax
from jax.experimental import pallas as pl
from jax.experimental.pallas import tpu as pltpu
from jax.sharding import PartitionSpec as P

BLOCK = 128
MOVE = 512
TAIL = 4 * MOVE // BLOCK
UNROLL = 32
MESH = pl.DeviceIdType.MESH
BF = jnp.bfloat16
F32 = jnp.float32

step_size = 0.25
ALPHA = 0.5 * math.log2(math.e)
ROOT = math.sqrt(ALPHA)
CUT = 9.0 * ALPHA
SOFT = 0.05 * ALPHA
KICK = step_size / math.sqrt(BLOCK)
SCALE = ALPHA**1.5 * 2.0**-CUT / CUT**2 / ROOT * KICK


def split3(value):
    high = value.astype(BF).astype(F32)
    rest = value - high
    middle = rest.astype(BF).astype(F32)
    return high, middle, rest - middle


def neighbour(k):
    n_dom = lax.axis_size("dom")
    offset = (1, n_dom - 1, n_dom // 4, n_dom - n_dom // 4)[k]
    return lax.rem(lax.axis_index("dom") + offset, n_dom)


def greet():
    barrier = pltpu.get_barrier_semaphore()
    pl.semaphore_signal(barrier, inc=1, device_id={"slab": 1 - lax.axis_index("slab")}, device_id_type=MESH)
    for k in range(4):
        pl.semaphore_signal(barrier, inc=1, device_id={"dom": neighbour(k)}, device_id_type=MESH)
    pl.semaphore_wait(barrier, 5)


def exchange_kernel(
    pos_ref, vel_ref, dest_ref, live_ref, ghost_ref,
    own_ref, part_ref, gho_ref, vout_ref,
    rhs, ranks, rows, moved, landed, gbuf, send, recv,
):
    n_groups = dest_ref.shape[0]
    partner = {"slab": 1 - lax.axis_index("slab")}
    live = live_ref[0]

    def codes_of(start, size):
        codes = dest_ref[pl.ds(start, size), :]
        slot = (start + lax.broadcasted_iota(jnp.int32, (size, 128), 0)) * 128
        slot = slot + lax.broadcasted_iota(jnp.int32, (size, 128), 1)
        return jnp.where(slot < live, codes, -1)

    row16 = lax.broadcasted_iota(jnp.int32, (16, 128), 0)

    def drift(i, _):
        base = pl.multiple_of(i * 16, 16)
        stay = jnp.where(codes_of(base, 16) == 0, 1.0, 0.0)
        for u in range(16):
            lanes = pl.ds(pl.multiple_of((base + u) * 128, 128), 128)
            p = pos_ref[:, lanes]
            v = vel_ref[:, lanes]
            here = stay[u : u + 1]
            own_ref[base + u, 0:3, :] = (p + step_size * v) * here
            own_ref[base + u, 3:4, :] = here
            vout_ref[base + u] = v * here
        for c in range(3):
            p = jnp.zeros((16, 128), F32)
            v = jnp.zeros((16, 128), F32)
            for u in range(16):
                lanes = pl.ds(pl.multiple_of((base + u) * 128, 128), 128)
                p = jnp.where(row16 == u, pos_ref[c : c + 1, lanes], p)
                v = jnp.where(row16 == u, vel_ref[c : c + 1, lanes], v)
            for f, value in ((c, p + step_size * v), (c + 3, v)):
                for piece, part in enumerate(split3(value)):
                    at = (f * 3 + piece) * 128
                    rhs[pl.ds(base, 16), at : at + 128] = part.astype(BF)
        return 0

    lax.fori_loop(0, n_groups // 16, drift, 0)
    greet()

    def remote(source, target, slot, device):
        return pltpu.make_async_remote_copy(
            src_ref=source,
            dst_ref=target,
            send_sem=send.at[slot],
            recv_sem=recv.at[slot],
            device_id=device,
            device_id_type=MESH,
        )

    body = remote(own_ref.at[pl.ds(0, n_groups)], part_ref.at[pl.ds(0, n_groups)], 0, partner)
    body.start()

    codes = codes_of(0, n_groups)
    lane_r = lax.broadcasted_iota(jnp.int32, (128, 256), 0)
    lane_c = lax.broadcasted_iota(jnp.int32, (128, 256), 1)
    inside_w = jnp.where(lane_r <= lane_c, 1.0, 0.0).astype(BF)
    group_r = lax.broadcasted_iota(jnp.int32, (n_groups, n_groups), 0)
    group_c = lax.broadcasted_iota(jnp.int32, (n_groups, n_groups), 1)
    before_w = jnp.where(group_c < group_r, 1.0, 0.0).astype(BF)
    for k in range(4):
        moving = codes == k + 1
        counted = jnp.dot(jnp.where(moving, 1.0, 0.0).astype(BF), inside_w, preferred_element_type=F32)
        total = counted[:, 128:]
        before = jnp.dot(before_w, total.astype(BF), preferred_element_type=F32)
        rank = (counted[:, :128] + before).astype(jnp.int32) - 1
        ranks[k] = jnp.where(moving, (rank & 127) + 1, 0).astype(F32).astype(BF)
        first = before.T[0:8]
        rows[k, 0:8, :] = first
        rows[k, 8:16, :] = first + total.T[0:8]

    slot_col = lax.broadcasted_iota(jnp.int32, (256, n_groups), 0).astype(F32)
    wanted = ((lax.broadcasted_iota(jnp.int32, (256, 128), 0) & 127) + 1).astype(F32)
    column = lax.broadcasted_iota(jnp.int32, (128, 128), 1)

    def unit(c):
        return jnp.where(column == c, 1.0, 0.0).astype(BF)

    def gather(i, _):
        k = i // 2
        half = i % 2
        at = slot_col + (half * 256).astype(F32)
        hot = jnp.where((at >= rows[k, 0:1, :]) & (at < rows[k, 8:9, :]), 1.0, 0.0).astype(BF)
        match = jnp.dot(hot, ranks[k], preferred_element_type=F32) == wanted
        total = jnp.dot(jnp.where(match, 1.0, 0.0).astype(BF), unit(3), preferred_element_type=F32)
        for f in range(6):
            target = unit(f if f < 3 else f + 1)
            parts = jnp.dot(hot, rhs[:, f * 384 : f * 384 + 384], preferred_element_type=F32)
            chosen = [jnp.where(match, parts[:, 128 * q : 128 * q + 128], 0.0).astype(BF) for q in range(3)]
            total = total + jnp.dot(
                jnp.concatenate(chosen, axis=1),
                jnp.concatenate([target] * 3, axis=0),
                preferred_element_type=F32,
            )
        turned = total.T
        moved[2 * i] = turned[0:8, 0:128]
        moved[2 * i + 1] = turned[0:8, 128:256]
        return 0

    lax.fori_loop(0, 8, gather, 0)
    per = MOVE // BLOCK
    movers = []
    for k in range(4):
        there = pl.ds(per * k, per)
        movers.append(remote(moved.at[there], landed.at[there], 1 + k, {"dom": neighbour(k)}))
        movers[-1].start()
    for copy in movers:
        copy.wait()
    for j in range(TAIL):
        own_ref[n_groups + j] = landed[j, 0:4, :]
        vout_ref[n_groups + j] = landed[j, 4:7, :]
    tail_at = pl.ds(n_groups, TAIL)
    tail = remote(own_ref.at[tail_at], part_ref.at[tail_at], 5, partner)
    tail.start()

    def pick(i, _):
        for u in range(8):
            gbuf[8 * i + u] = own_ref[ghost_ref[8 * i + u]]
        return 0

    n_ghost = gbuf.shape[0]
    lax.fori_loop(0, n_ghost // 8, pick, 0)
    ghosts = []
    for k in range(4):
        there = pl.ds(n_ghost // 4 * k, n_ghost // 4)
        ghosts.append(remote(gbuf.at[there], gho_ref.at[there], 6 + k, {"dom": neighbour(k)}))
        ghosts[-1].start()
    for copy in ghosts:
        copy.wait()
    body.wait()
    tail.wait()


def features(block, row):
    pos = jnp.where(row < 3, jnp.concatenate([block, jnp.zeros_like(block)], axis=0) * ROOT, 0.0)
    return pos, jnp.sum(pos * pos, axis=0, keepdims=True), block[3:4]


def pair_kernel(pairs_ref, count_ref, own_ref, part_ref, gho_ref, acc_ref, pool, sems):
    n_own = own_ref.shape[0]
    copies = []
    start = 0
    for i, ref in enumerate((own_ref, part_ref, gho_ref)):
        copies.append(pltpu.make_async_copy(ref, pool.at[pl.ds(start, ref.shape[0])], sems.at[i]))
        copies[-1].start()
        start += ref.shape[0]
    acc_ref[...] = jnp.zeros_like(acc_ref)
    for copy in copies:
        copy.wait()
    row = lax.broadcasted_iota(jnp.int32, (8, 128), 0)
    lane = lax.broadcasted_iota(jnp.int32, (128, 128), 1)
    count = count_ref[0]
    npair = pairs_ref.shape[0] // 2
    blank = jnp.zeros((8, 128), F32)

    def group(p0):
        items, fars = [], []
        for u in range(4):
            p = p0 + u
            a = pairs_ref[p]
            b = pairs_ref[npair + p]
            pa, na, wa = features(pool[a], row)
            pb, nb, wb = features(pool[b], row)
            near = jnp.where(row < 3, 2.0 * pa, jnp.where(row == 3, -1.0, jnp.where(row == 4, CUT - na, jnp.where(row == 5, wa, 0.0))))
            far = jnp.where(row < 3, pb, jnp.where(row == 3, nb, jnp.where(row == 4, 1.0, jnp.where(row == 7, wb, 0.0))))
            ah, am, al = split3(near)
            bh, bm, bl = split3(far)
            left = jnp.concatenate([ah, ah, ah, am, am, al], axis=0)
            right = jnp.concatenate([bh, bm, bl, bh, bm, bh], axis=0).astype(BF)
            near_f = jnp.concatenate([ah, am, al, blank], axis=0).astype(BF)
            fars += [bh, bm, bl, blank]
            items.append((p, a, b, pa, wa, pb, wb, left, right, near_f))
        far_t = jnp.concatenate(fars, axis=0).T.astype(BF)
        out, strengths, weights = [], [], []
        for u, (p, a, b, pa, wa, pb, wb, left, right, near_f) in enumerate(items):
            raw = jnp.dot(left.T.astype(BF), right, preferred_element_type=F32)
            taper = jnp.maximum(raw, 0.0)
            inv = lax.rsqrt((CUT + SOFT) - raw)
            ratio = taper * inv
            s = (ratio * ratio) * (inv * jnp.exp2(taper))
            high = s.astype(BF)
            low = (s - high.astype(F32)).astype(BF)
            mine = jnp.where((lane >= 32 * u) & (lane < 32 * u + 32), far_t, jnp.zeros_like(far_t))
            strengths += [high, low]
            weights += [mine, mine]
            g = jnp.dot(
                jnp.concatenate([near_f, near_f], axis=1),
                jnp.concatenate([high, low], axis=0),
                preferred_element_type=F32,
            )
            g = g[0:8] + g[8:16] + g[16:24]
            on = jnp.where(p < count, SCALE, 0.0)
            out.append([a, b, None, ((0.5 * g - pb * g[5:6]) * (wb * on))[:4]])
        g_near = jnp.dot(
            jnp.concatenate(strengths, axis=1),
            jnp.concatenate(weights, axis=0),
            preferred_element_type=F32,
        ).T
        for u, (p, a, b, pa, wa, pb, wb, left, right, near_f) in enumerate(items):
            g = g_near[32 * u : 32 * u + 8] + g_near[32 * u + 8 : 32 * u + 16] + g_near[32 * u + 16 : 32 * u + 24]
            on = jnp.where(p < count, SCALE, 0.0)
            out[u][2] = ((g - pa * g[7:8]) * (wa * on))[:4]
        return out

    def turn(t, _):
        found = []
        for g in range(UNROLL // 4):
            found += group(t * UNROLL + 4 * g)
        for a, b, on_near, on_far in found:
            acc_ref[a] += on_near
            acc_ref[b] += on_far
        return 0

    lax.fori_loop(0, (count + UNROLL - 1) // UNROLL, turn, 0)


def return_kernel(acc_ref, pret_ref, gret_ref, send, recv):
    n_own = pret_ref.shape[0]
    per = gret_ref.shape[0] // 4
    greet()
    copies = [
        pltpu.make_async_remote_copy(
            src_ref=acc_ref.at[pl.ds(n_own, n_own)],
            dst_ref=pret_ref,
            send_sem=send.at[0],
            recv_sem=recv.at[0],
            device_id={"slab": 1 - lax.axis_index("slab")},
            device_id_type=MESH,
        )
    ]
    for k in range(4):
        copies.append(
            pltpu.make_async_remote_copy(
                src_ref=acc_ref.at[pl.ds(2 * n_own + per * k, per)],
                dst_ref=gret_ref.at[pl.ds(per * k, per)],
                send_sem=send.at[1 + k],
                recv_sem=recv.at[1 + k],
                device_id={"dom": neighbour(k ^ 1)},
                device_id_type=MESH,
            )
        )
    for copy in copies:
        copy.start()
    for copy in copies:
        copy.wait()


def finish_kernel(ghost_ref, own_ref, vel_ref, acc_ref, pret_ref, gret_ref, npos_ref, nvel_ref, total):
    n_own = own_ref.shape[0]
    total[...] = acc_ref[...] + pret_ref[...]

    def back(i, _):
        for u in range(8):
            total[ghost_ref[8 * i + u]] += gret_ref[8 * i + u]
        return 0

    lax.fori_loop(0, gret_ref.shape[0] // 8, back, 0)

    def write(i, _):
        for u in range(16):
            b = i * 16 + u
            lanes = pl.ds(pl.multiple_of(b * 128, 128), 128)
            npos_ref[:, lanes] = own_ref[b, 0:3, :]
            nvel_ref[:, lanes] = vel_ref[b] + total[b, 0:3, :]
        return 0

    lax.fori_loop(0, n_own // 16, write, 0)


def shards(positions, velocities, destination, live_count, ghost_list, pair_blocks, pair_count):
    n_rows = positions.shape[1]
    n_groups = n_rows // BLOCK
    n_own = n_groups + TAIL
    n_ghost = 4 * ghost_list.shape[2]
    n_pool = 2 * n_own + n_ghost
    smem = pl.BlockSpec(memory_space=pltpu.SMEM)
    vmem = pl.BlockSpec(memory_space=pltpu.VMEM)
    anywhere = pl.BlockSpec(memory_space=pl.ANY)
    ghost_flat = ghost_list.reshape(n_ghost)
    pairs = pair_blocks[0].T.reshape(2 * pair_blocks.shape[1])

    own, part, gho, vel = pl.pallas_call(
        exchange_kernel,
        out_shape=(
            jax.ShapeDtypeStruct((n_own, 4, BLOCK), F32),
            jax.ShapeDtypeStruct((n_own, 4, BLOCK), F32),
            jax.ShapeDtypeStruct((n_ghost, 4, BLOCK), F32),
            jax.ShapeDtypeStruct((n_own, 3, BLOCK), F32),
        ),
        in_specs=[vmem, vmem, vmem, smem, smem],
        out_specs=(vmem, vmem, vmem, vmem),
        scratch_shapes=[
            pltpu.VMEM((n_groups, 18 * BLOCK), BF),
            pltpu.VMEM((4, n_groups, BLOCK), BF),
            pltpu.VMEM((4, 16, n_groups), F32),
            pltpu.VMEM((TAIL, 8, BLOCK), F32),
            pltpu.VMEM((TAIL, 8, BLOCK), F32),
            pltpu.VMEM((n_ghost, 4, BLOCK), F32),
            pltpu.SemaphoreType.DMA((10,)),
            pltpu.SemaphoreType.DMA((10,)),
        ],
        compiler_params=pltpu.CompilerParams(
            collective_id=0, has_side_effects=True, vmem_limit_bytes=48 << 20
        ),
        name="exchange",
    )(positions, velocities, destination.reshape(n_groups, BLOCK), live_count, ghost_flat)

    acc = pl.pallas_call(
        pair_kernel,
        out_shape=jax.ShapeDtypeStruct((n_pool, 4, BLOCK), F32),
        in_specs=[smem, smem, anywhere, anywhere, anywhere],
        out_specs=vmem,
        scratch_shapes=[
            pltpu.VMEM((n_pool, 4, BLOCK), F32),
            pltpu.SemaphoreType.DMA((3,)),
        ],
        compiler_params=pltpu.CompilerParams(vmem_limit_bytes=48 << 20),
        name="pairs",
    )(pairs, pair_count, own, part, gho)

    pret, gret = pl.pallas_call(
        return_kernel,
        out_shape=(
            jax.ShapeDtypeStruct((n_own, 4, BLOCK), F32),
            jax.ShapeDtypeStruct((n_ghost, 4, BLOCK), F32),
        ),
        in_specs=[anywhere],
        out_specs=(anywhere, anywhere),
        scratch_shapes=[pltpu.SemaphoreType.DMA((5,)), pltpu.SemaphoreType.DMA((5,))],
        compiler_params=pltpu.CompilerParams(collective_id=1, has_side_effects=True),
        name="returns",
    )(acc)

    whole = lambda *shape: pl.BlockSpec(shape, lambda i: (0,) * len(shape))
    return pl.pallas_call(
        finish_kernel,
        grid=(1,),
        out_shape=(
            jax.ShapeDtypeStruct((3, n_own * BLOCK), F32),
            jax.ShapeDtypeStruct((3, n_own * BLOCK), F32),
        ),
        in_specs=[
            smem,
            whole(n_own, 4, BLOCK),
            whole(n_own, 3, BLOCK),
            whole(n_own, 4, BLOCK),
            whole(n_own, 4, BLOCK),
            whole(n_ghost, 4, BLOCK),
        ],
        out_specs=(whole(3, n_own * BLOCK), whole(3, n_own * BLOCK)),
        scratch_shapes=[pltpu.VMEM((n_own, 4, BLOCK), F32)],
        compiler_params=pltpu.CompilerParams(vmem_limit_bytes=48 << 20),
        name="finish",
    )(ghost_flat, own, vel, acc, pret, gret)


def solution(mesh):
    return jax.shard_map(
        shards,
        mesh=mesh,
        in_specs=(
            P(None, ("dom", "slab")),
            P(None, ("dom", "slab")),
            P(("dom", "slab")),
            P(("dom", "slab")),
            P(("dom", "slab"), None, None),
            P(("dom", "slab"), None, None),
            P(("dom", "slab")),
        ),
        out_specs=(P(None, ("dom", "slab")), P(None, ("dom", "slab"))),
        check_vma=False,
    )
```

```python
import functools
import math

import jax
import jax.numpy as jnp
from jax import lax
from jax.experimental import pallas as pl
from jax.experimental.pallas import tpu as pltpu
from jax.sharding import PartitionSpec as P

BLOCK = 128
MOVE = 512
TAIL = 4 * MOVE // BLOCK
GROUP = 8
MESH = pl.DeviceIdType.MESH
BF = jnp.bfloat16
F32 = jnp.float32

step_size = 0.25
ALPHA = 0.5 * math.log2(math.e)
ROOT = math.sqrt(ALPHA)
CUT = 9.0 * ALPHA
SOFT = 0.05 * ALPHA
KICK = step_size / math.sqrt(BLOCK)
SCALE = ALPHA**1.5 * 2.0**-CUT / CUT**2 / ROOT * KICK


def split3(value):
    high = value.astype(BF).astype(F32)
    rest = value - high
    middle = rest.astype(BF).astype(F32)
    return high, middle, rest - middle


def neighbour(k):
    n_dom = lax.axis_size("dom")
    offset = (1, n_dom - 1, n_dom // 4, n_dom - n_dom // 4)[k]
    return lax.rem(lax.axis_index("dom") + offset, n_dom)


def greet():
    barrier = pltpu.get_barrier_semaphore()
    pl.semaphore_signal(barrier, inc=1, device_id={"slab": 1 - lax.axis_index("slab")}, device_id_type=MESH)
    for k in range(4):
        pl.semaphore_signal(barrier, inc=1, device_id={"dom": neighbour(k)}, device_id_type=MESH)
    pl.semaphore_wait(barrier, 5)


def exchange_kernel(
    pos_hbm, vel_hbm, dest_hbm, live_ref, ghost_ref,
    pool_ref, vout_ref,
    pos_ref, vel_ref, dest_ref, own, main, extra, ranks, spans, moved, landed, gbuf, local, send, recv,
):
    n_groups = dest_ref.shape[0]
    n_own = own.shape[0]
    n_ghost = gbuf.shape[0]
    partner = {"slab": 1 - lax.axis_index("slab")}
    live = live_ref[0]
    loads = []
    for i, (source, target) in enumerate(((dest_hbm, dest_ref), (pos_hbm, pos_ref), (vel_hbm, vel_ref))):
        loads.append(pltpu.make_async_copy(source, target, local.at[i]))
        loads[-1].start()
    greet()

    def codes_of(start, size):
        codes = dest_ref[pl.ds(start, size), :]
        slot = (start + lax.broadcasted_iota(jnp.int32, (size, 128), 0)) * 128
        slot = slot + lax.broadcasted_iota(jnp.int32, (size, 128), 1)
        return jnp.where(slot < live, codes, -1)

    row16 = lax.broadcasted_iota(jnp.int32, (16, 128), 0)

    def drift(i, _):
        base = pl.multiple_of(i * 16, 16)
        stay = jnp.where(codes_of(base, 16) == 0, 1.0, 0.0)
        for u in range(16):
            lanes = pl.ds(pl.multiple_of((base + u) * 128, 128), 128)
            p = pos_ref[:, lanes]
            v = vel_ref[:, lanes]
            here = stay[u : u + 1]
            kept = (p + step_size * v) * here
            own[base + u, 0:3, :] = kept
            own[base + u, 3:4, :] = here
            pool_ref[base + u, 0:3, :] = kept
            pool_ref[base + u, 3:4, :] = here
            vout_ref[base + u] = v * here
        for c in range(3):
            p = jnp.zeros((16, 128), F32)
            v = jnp.zeros((16, 128), F32)
            for u in range(16):
                lanes = pl.ds(pl.multiple_of((base + u) * 128, 128), 128)
                p = jnp.where(row16 == u, pos_ref[c : c + 1, lanes], p)
                v = jnp.where(row16 == u, vel_ref[c : c + 1, lanes], v)
            high, middle, low = split3(p + step_size * v)
            main[c, pl.ds(base, 16), 0:128] = high.astype(BF)
            main[c, pl.ds(base, 16), 128:256] = middle.astype(BF)
            extra[c, pl.ds(base, 16), :] = low.astype(BF)
            high, middle, _ = split3(v)
            main[3 + c, pl.ds(base, 16), 0:128] = high.astype(BF)
            main[3 + c, pl.ds(base, 16), 128:256] = middle.astype(BF)
        return 0

    for load in loads:
        load.wait()
    lax.fori_loop(0, n_groups // 16, drift, 0)

    def remote(source, target, slot, device):
        return pltpu.make_async_remote_copy(
            src_ref=source,
            dst_ref=target,
            send_sem=send.at[slot],
            recv_sem=recv.at[slot],
            device_id=device,
            device_id_type=MESH,
        )

    body = remote(own.at[pl.ds(0, n_groups)], pool_ref.at[pl.ds(n_own, n_groups)], 0, partner)
    body.start()

    codes = codes_of(0, n_groups)
    lane_r = lax.broadcasted_iota(jnp.int32, (128, 256), 0)
    lane_c = lax.broadcasted_iota(jnp.int32, (128, 256), 1)
    inside_w = jnp.where(lane_r <= lane_c, 1.0, 0.0).astype(BF)
    group_r = lax.broadcasted_iota(jnp.int32, (n_groups, n_groups), 0)
    group_c = lax.broadcasted_iota(jnp.int32, (n_groups, n_groups), 1)
    before_w = jnp.where(group_c < group_r, 1.0, 0.0).astype(BF)
    for k in range(4):
        moving = codes == k + 1
        counted = jnp.dot(jnp.where(moving, 1.0, 0.0).astype(BF), inside_w, preferred_element_type=F32)
        total = counted[:, 128:]
        before = jnp.dot(before_w, total.astype(BF), preferred_element_type=F32)
        rank = (counted[:, :128] + before).astype(jnp.int32) - 1
        ranks[k] = jnp.where(moving, (rank & 127) + 1, 0).astype(F32).astype(BF).T
        spans[k, 0] = before
        spans[k, 1] = before + total

    slot = lax.broadcasted_iota(jnp.int32, (n_groups, 256), 1).astype(F32)
    wanted = ((lax.broadcasted_iota(jnp.int32, (128, 256), 1) & 127) + 1).astype(F32)

    def gather(i, _):
        k = i // 2
        at = slot + ((i % 2) * 256).astype(F32)
        first, last = spans[k, 0], spans[k, 1]
        here = (at >= jnp.concatenate([first, first], axis=1)) & (at < jnp.concatenate([last, last], axis=1))
        hot = jnp.where(here, 1.0, 0.0)
        found = jnp.dot(ranks[k], hot.astype(BF), preferred_element_type=F32)
        lane = jnp.where(found == wanted, 1.0, 0.0).astype(BF)
        twice = jnp.concatenate([lane, lane], axis=0)

        def put(f, value):
            moved[2 * i, f : f + 1, :] = value[:, :128]
            moved[2 * i + 1, f : f + 1, :] = value[:, 128:]

        for f in range(6):
            fields = jnp.dot(main[f], twice, preferred_element_type=F32)
            if f < 3:
                fields = fields + jnp.dot(extra[f], lane, preferred_element_type=F32)
            put(f if f < 3 else f + 1, jnp.sum(jnp.where(here, fields, 0.0), axis=0, keepdims=True))
        put(3, jnp.sum(hot, axis=0, keepdims=True))
        put(7, jnp.zeros((1, 256), F32))
        return 0

    lax.fori_loop(0, 8, gather, 0)
    per = MOVE // BLOCK
    movers = []
    for k in range(4):
        there = pl.ds(per * k, per)
        movers.append(remote(moved.at[there], landed.at[there], 1 + k, {"dom": neighbour(k)}))
        movers[-1].start()
    for copy in movers:
        copy.wait()
    for j in range(TAIL):
        own[n_groups + j] = landed[j, 0:4, :]
        pool_ref[n_groups + j] = landed[j, 0:4, :]
        vout_ref[n_groups + j] = landed[j, 4:7, :]
    tail = remote(own.at[pl.ds(n_groups, TAIL)], pool_ref.at[pl.ds(n_own + n_groups, TAIL)], 5, partner)
    tail.start()
    per = n_ghost // 4
    ghosts = []
    for k in range(4):

        def pick(i, _):
            for u in range(8):
                gbuf[per * k + 8 * i + u] = own[ghost_ref[k, 8 * i + u]]
            return 0

        lax.fori_loop(0, per // 8, pick, 0)
        there = pl.ds(2 * n_own + per * k, per)
        ghosts.append(remote(gbuf.at[pl.ds(per * k, per)], pool_ref.at[there], 6 + k, {"dom": neighbour(k)}))
        ghosts[-1].start()
    for copy in ghosts:
        copy.wait()
    body.wait()
    tail.wait()


def features(block, row):
    pos = jnp.where(row < 3, jnp.concatenate([block, jnp.zeros_like(block)], axis=0) * ROOT, 0.0)
    return pos, jnp.sum(pos * pos, axis=0, keepdims=True), block[3:4]


def pair_kernel(pairs_ref, count_ref, pool, acc_ref, lefts, rights, nears, highs, lows):
    acc_ref[...] = jnp.zeros_like(acc_ref)
    rights[...] = jnp.zeros_like(rights)
    row = lax.broadcasted_iota(jnp.int32, (8, 128), 0)
    count = count_ref[0]
    npair = pairs_ref.shape[1]

    def cat(parts, axis):
        return jnp.concatenate(parts, axis=axis)

    def blocks_of(p):
        p = jnp.clip(p, 0, npair - 1)
        return pairs_ref[0, p], pairs_ref[1, p]

    def prepare(t, slot):
        left = []
        for u in range(GROUP):
            a, b = blocks_of(t * GROUP + u)
            pa, na, wa = features(pool[a], row)
            pb, nb, wb = features(pool[b], row)
            near = jnp.where(row < 3, 2.0 * pa, jnp.where(row == 3, -1.0, jnp.where(row == 4, CUT - na, jnp.where(row == 5, wa, 0.0))))
            far = jnp.where(row < 3, pb, jnp.where(row == 3, nb, jnp.where(row == 4, 1.0, jnp.where(row == 7, wb, 0.0))))
            ah, am, al = split3(near)
            bh, bm, bl = split3(far)
            v = u % 2
            left.append(cat([ah, ah, ah, am, am, al], 0).astype(BF))
            right = cat([bh, bm, bl, bh, bm, bh], 0).astype(BF)
            rights[slot, u // 2, 48 * v : 48 * v + 48, 128 * v : 128 * v + 128] = right
            nears[slot, u] = cat([ah, am, al, bh, bm, bl], 0).astype(BF)
        for c in range(GROUP // 2):
            lefts[slot, c] = cat(left[2 * c : 2 * c + 2], 0).T

    def strengths(slot):
        for c in range(GROUP // 2):
            raw = jnp.dot(lefts[slot, c], rights[slot, c], preferred_element_type=F32)
            inv = lax.rsqrt((CUT + SOFT) - raw)
            ratio = jnp.maximum(raw, 0.0) * inv
            s = (ratio * ratio) * (inv * jnp.exp2(raw))
            high = s.astype(BF)
            highs[slot, :, 256 * c : 256 * c + 256] = high
            lows[slot, :, 256 * c : 256 * c + 256] = (s - high.astype(F32)).astype(BF)

    def sums(t, slot):
        found = []
        for u in range(GROUP):
            p = t * GROUP + u
            a, b = blocks_of(p)
            xa, xb = pool[a], pool[b]
            lanes = slice(128 * u, 128 * u + 128)
            high, low = highs[slot, :, lanes], lows[slot, :, lanes]
            f = nears[slot, u]
            both = jnp.dot(
                cat([f, f], 1),
                cat([cat([high, high.T], 1), cat([low, low.T], 1)], 0),
                preferred_element_type=F32,
            )
            g = both[0:8, :128] + both[8:16, :128] + both[16:24, :128]
            h = both[24:32, 128:] + both[32:40, 128:] + both[40:48, 128:]
            on = (p >= 0) & (p < count)
            on_far = (0.5 * g[:4] - (ROOT * xb) * g[5:6]) * (SCALE * xb[3:4])
            on_near = (h[:4] - (ROOT * xa) * h[7:8]) * (SCALE * xa[3:4])
            found.append((a, b, jnp.where(on, on_near, 0.0), jnp.where(on, on_far, 0.0)))
        for a, b, on_near, on_far in found:
            acc_ref[a] += on_near
            acc_ref[b] += on_far

    def turn(i, _):
        for v in range(3):
            t = 3 * i + v
            prepare(t, v)
            strengths((v + 2) % 3)
            sums(t - 2, (v + 1) % 3)
        return 0

    steps = (count + GROUP - 1) // GROUP + 2
    lax.fori_loop(0, (steps + 2) // 3, turn, 0)


def return_kernel(acc_ref, pret_ref, gret_ref, send, recv):
    n_own = pret_ref.shape[0]
    per = gret_ref.shape[0] // 4
    greet()
    copies = [
        pltpu.make_async_remote_copy(
            src_ref=acc_ref.at[pl.ds(n_own, n_own)],
            dst_ref=pret_ref,
            send_sem=send.at[0],
            recv_sem=recv.at[0],
            device_id={"slab": 1 - lax.axis_index("slab")},
            device_id_type=MESH,
        )
    ]
    for k in range(4):
        copies.append(
            pltpu.make_async_remote_copy(
                src_ref=acc_ref.at[pl.ds(2 * n_own + per * k, per)],
                dst_ref=gret_ref.at[pl.ds(per * k, per)],
                send_sem=send.at[1 + k],
                recv_sem=recv.at[1 + k],
                device_id={"dom": neighbour(k ^ 1)},
                device_id_type=MESH,
            )
        )
    for copy in copies:
        copy.start()
    for copy in copies:
        copy.wait()


def finish_kernel(ghost_ref, pool_ref, vel_ref, acc_ref, pret_ref, gret_ref, npos_ref, nvel_ref, total):
    n_own = vel_ref.shape[0]
    per = ghost_ref.shape[1]
    total[...] = acc_ref[0:n_own] + pret_ref[...]

    def back(i, _):
        for k in range(4):
            for u in range(4):
                total[ghost_ref[k, 4 * i + u]] += gret_ref[per * k + 4 * i + u]
        return 0

    lax.fori_loop(0, per // 4, back, 0)

    def write(i, _):
        for u in range(16):
            b = i * 16 + u
            lanes = pl.ds(pl.multiple_of(b * 128, 128), 128)
            npos_ref[:, lanes] = pool_ref[b, 0:3, :]
            nvel_ref[:, lanes] = vel_ref[b] + total[b, 0:3, :]
        return 0

    lax.fori_loop(0, n_own // 16, write, 0)


def shards(positions, velocities, destination, live_count, ghost_list, pair_blocks, pair_count):
    n_rows = positions.shape[1]
    n_groups = n_rows // BLOCK
    n_own = n_groups + TAIL
    n_ghost = 4 * ghost_list.shape[2]
    n_pool = 2 * n_own + n_ghost
    smem = pl.BlockSpec(memory_space=pltpu.SMEM)
    vmem = pl.BlockSpec(memory_space=pltpu.VMEM)
    anywhere = pl.BlockSpec(memory_space=pl.ANY)
    ghosts = ghost_list[0]
    pairs = pair_blocks[0].T

    pool, vel = pl.pallas_call(
        exchange_kernel,
        out_shape=(
            jax.ShapeDtypeStruct((n_pool, 4, BLOCK), F32),
            jax.ShapeDtypeStruct((n_own, 3, BLOCK), F32),
        ),
        in_specs=[anywhere, anywhere, anywhere, smem, smem],
        out_specs=(vmem, vmem),
        scratch_shapes=[
            pltpu.VMEM((3, n_rows), F32),
            pltpu.VMEM((3, n_rows), F32),
            pltpu.VMEM((n_groups, BLOCK), jnp.int32),
            pltpu.VMEM((n_own, 4, BLOCK), F32),
            pltpu.VMEM((6, n_groups, 2 * BLOCK), BF),
            pltpu.VMEM((3, n_groups, BLOCK), BF),
            pltpu.VMEM((4, BLOCK, n_groups), BF),
            pltpu.VMEM((4, 2, n_groups, BLOCK), F32),
            pltpu.VMEM((TAIL, 8, BLOCK), F32),
            pltpu.VMEM((TAIL, 8, BLOCK), F32),
            pltpu.VMEM((n_ghost, 4, BLOCK), F32),
            pltpu.SemaphoreType.DMA((3,)),
            pltpu.SemaphoreType.DMA((10,)),
            pltpu.SemaphoreType.DMA((10,)),
        ],
        compiler_params=pltpu.CompilerParams(
            collective_id=0, has_side_effects=True, vmem_limit_bytes=32 << 20
        ),
        name="exchange",
    )(positions, velocities, destination.reshape(n_groups, BLOCK), live_count, ghosts)

    acc = pl.pallas_call(
        pair_kernel,
        out_shape=jax.ShapeDtypeStruct((n_pool, 4, BLOCK), F32),
        in_specs=[smem, smem, vmem],
        out_specs=vmem,
        scratch_shapes=[
            pltpu.VMEM((3, GROUP // 2, BLOCK, 96), BF),
            pltpu.VMEM((3, GROUP // 2, 96, 2 * BLOCK), BF),
            pltpu.VMEM((3, GROUP, 48, BLOCK), BF),
            pltpu.VMEM((3, BLOCK, GROUP * BLOCK), BF),
            pltpu.VMEM((3, BLOCK, GROUP * BLOCK), BF),
        ],
        compiler_params=pltpu.CompilerParams(vmem_limit_bytes=32 << 20),
        name="pairs",
    )(pairs, pair_count, pool)

    pret, gret = pl.pallas_call(
        return_kernel,
        out_shape=(
            jax.ShapeDtypeStruct((n_own, 4, BLOCK), F32),
            jax.ShapeDtypeStruct((n_ghost, 4, BLOCK), F32),
        ),
        in_specs=[vmem],
        out_specs=(vmem, vmem),
        scratch_shapes=[pltpu.SemaphoreType.DMA((5,)), pltpu.SemaphoreType.DMA((5,))],
        compiler_params=pltpu.CompilerParams(
            collective_id=1, has_side_effects=True, vmem_limit_bytes=16 << 20
        ),
        name="returns",
    )(acc)

    return pl.pallas_call(
        finish_kernel,
        out_shape=(
            jax.ShapeDtypeStruct((3, n_own * BLOCK), F32),
            jax.ShapeDtypeStruct((3, n_own * BLOCK), F32),
        ),
        in_specs=[smem, vmem, vmem, vmem, vmem, vmem],
        out_specs=(vmem, vmem),
        scratch_shapes=[pltpu.VMEM((n_own, 4, BLOCK), F32)],
        compiler_params=pltpu.CompilerParams(vmem_limit_bytes=32 << 20),
        name="finish",
    )(ghosts, pool, vel, acc, pret, gret)


def solution(mesh):
    return jax.shard_map(
        shards,
        mesh=mesh,
        in_specs=(
            P(None, ("dom", "slab")),
            P(None, ("dom", "slab")),
            P(("dom", "slab")),
            P(("dom", "slab")),
            P(("dom", "slab"), None, None),
            P(("dom", "slab"), None, None),
            P(("dom", "slab")),
        ),
        out_specs=(P(None, ("dom", "slab")), P(None, ("dom", "slab"))),
        check_vma=False,
    )
```

```python
import functools
import math

import jax
import jax.numpy as jnp
from jax import lax
from jax.experimental import pallas as pl
from jax.experimental.pallas import tpu as pltpu
from jax.sharding import PartitionSpec as P

BLOCK = 128
MOVE = 512
TAIL = 4 * MOVE // BLOCK
GROUP = 8
MESH = pl.DeviceIdType.MESH
BF = jnp.bfloat16
F32 = jnp.float32

step_size = 0.25
ALPHA = 0.5 * math.log2(math.e)
ROOT = math.sqrt(ALPHA)
CUT = 9.0 * ALPHA
SOFT = 0.05 * ALPHA
KICK = step_size / math.sqrt(BLOCK)
SCALE = ALPHA**1.5 * 2.0**-CUT / CUT**2 / ROOT * KICK


def split3(value):
    high = value.astype(BF).astype(F32)
    rest = value - high
    middle = rest.astype(BF).astype(F32)
    return high, middle, rest - middle


def neighbour(k):
    n_dom = lax.axis_size("dom")
    offset = (1, n_dom - 1, n_dom // 4, n_dom - n_dom // 4)[k]
    return lax.rem(lax.axis_index("dom") + offset, n_dom)


def greet():
    barrier = pltpu.get_barrier_semaphore()
    pl.semaphore_signal(barrier, inc=1, device_id={"slab": 1 - lax.axis_index("slab")}, device_id_type=MESH)
    for k in range(4):
        pl.semaphore_signal(barrier, inc=1, device_id={"dom": neighbour(k)}, device_id_type=MESH)
    pl.semaphore_wait(barrier, 5)


def exchange_kernel(
    pos_hbm, vel_hbm, dest_hbm, pairs_hbm, ghost_hbm, live_ref, count_ref,
    pool_ref, xst_ref, vst_ref, mine_ref, theirs_ref,
    pos_ref, vel_ref, dest_ref, pairs_ref, ghost_ref, own, drifted, speeds,
    main, extra, ranks, spans, moved, landed, gbuf, local, send, recv,
):
    n_groups = dest_ref.shape[0]
    n_own = own.shape[0]
    n_ghost = gbuf.shape[0]
    partner = {"slab": 1 - lax.axis_index("slab")}
    live = live_ref[0]
    loads = []
    for i, (source, target) in enumerate((
        (dest_hbm, dest_ref),
        (pos_hbm, pos_ref.at[0:3]),
        (vel_hbm, vel_ref.at[0:3]),
        (pairs_hbm, pairs_ref),
        (ghost_hbm, ghost_ref),
    )):
        loads.append(pltpu.make_async_copy(source, target, local.at[i]))
        loads[-1].start()
    greet()

    def codes_of(start, size):
        codes = dest_ref[pl.ds(start, size), :]
        slot = (start + lax.broadcasted_iota(jnp.int32, (size, 128), 0)) * 128
        slot = slot + lax.broadcasted_iota(jnp.int32, (size, 128), 1)
        return jnp.where(slot < live, codes, -1)

    row4 = lax.broadcasted_iota(jnp.int32, (4, 128), 0)

    def drift(i, _):
        base = pl.multiple_of(i * 16, 16)
        stay = jnp.where(codes_of(base, 16) == 0, 1.0, 0.0)
        for u in range(16):
            lanes = pl.ds(pl.multiple_of((base + u) * 128, 128), 128)
            rows = pl.ds(pl.multiple_of((base + u) * 8, 8), 4)
            v = vel_ref[:, lanes]
            x = pos_ref[:, lanes] + step_size * v
            here = stay[u : u + 1]
            own[base + u] = jnp.where(row4 == 3, 1.0, x) * here
            vst_ref[:, lanes] = v[0:3] * here
            drifted[rows, :] = x
            speeds[rows, :] = v
        for c in range(3):
            column = pl.ds(base * 8 + c, 16, stride=8)
            high, middle, low = split3(drifted[column, :])
            main[c, pl.ds(base, 16), 0:128] = high.astype(BF)
            main[c, pl.ds(base, 16), 128:256] = middle.astype(BF)
            extra[c, pl.ds(base, 16), :] = low.astype(BF)
            high, middle, _ = split3(speeds[column, :])
            main[3 + c, pl.ds(base, 16), 0:128] = high.astype(BF)
            main[3 + c, pl.ds(base, 16), 128:256] = middle.astype(BF)
        return 0

    for load in loads:
        load.wait()
    mine_ref[0:2, :] = pairs_ref[...]
    mine_ref[2:4, :] = jnp.full((2, mine_ref.shape[1]), count_ref[0], jnp.int32)
    lax.fori_loop(0, n_groups // 16, drift, 0)

    def remote(source, target, slot, device):
        return pltpu.make_async_remote_copy(
            src_ref=source,
            dst_ref=target,
            send_sem=send.at[slot],
            recv_sem=recv.at[slot],
            device_id=device,
            device_id_type=MESH,
        )

    body = remote(own.at[pl.ds(0, n_groups)], pool_ref.at[pl.ds(n_own, n_groups)], 0, partner)
    body.start()
    listed = remote(mine_ref, theirs_ref, 10, partner)
    listed.start()
    kept = pltpu.make_async_copy(own.at[pl.ds(0, n_groups)], pool_ref.at[pl.ds(0, n_groups)], local.at[5])
    kept.start()

    codes = codes_of(0, n_groups)
    lane_r = lax.broadcasted_iota(jnp.int32, (128, 256), 0)
    lane_c = lax.broadcasted_iota(jnp.int32, (128, 256), 1)
    inside_w = jnp.where(lane_r <= lane_c, 1.0, 0.0).astype(BF)
    group_r = lax.broadcasted_iota(jnp.int32, (n_groups, n_groups), 0)
    group_c = lax.broadcasted_iota(jnp.int32, (n_groups, n_groups), 1)
    before_w = jnp.where(group_c < group_r, 1.0, 0.0).astype(BF)
    for k in range(4):
        moving = codes == k + 1
        counted = jnp.dot(jnp.where(moving, 1.0, 0.0).astype(BF), inside_w, preferred_element_type=F32)
        total = counted[:, 128:]
        before = jnp.dot(before_w, total.astype(BF), preferred_element_type=F32)
        rank = (counted[:, :128] + before).astype(jnp.int32) - 1
        ranks[k] = jnp.where(moving, (rank & 127) + 1, 0).astype(F32).astype(BF).T
        spans[k, 0] = before
        spans[k, 1] = before + total

    slot = lax.broadcasted_iota(jnp.int32, (n_groups, 256), 1).astype(F32)
    wanted = ((lax.broadcasted_iota(jnp.int32, (128, 256), 1) & 127) + 1).astype(F32)

    def gather(i, _):
        k = i // 2
        at = slot + ((i % 2) * 256).astype(F32)
        first, last = spans[k, 0], spans[k, 1]
        here = (at >= jnp.concatenate([first, first], axis=1)) & (at < jnp.concatenate([last, last], axis=1))
        hot = jnp.where(here, 1.0, 0.0)
        found = jnp.dot(ranks[k], hot.astype(BF), preferred_element_type=F32)
        lane = jnp.where(found == wanted, 1.0, 0.0).astype(BF)
        twice = jnp.concatenate([lane, lane], axis=0)

        def put(f, value):
            moved[2 * i, f : f + 1, :] = value[:, :128]
            moved[2 * i + 1, f : f + 1, :] = value[:, 128:]

        for f in range(6):
            fields = jnp.dot(main[f], twice, preferred_element_type=F32)
            if f < 3:
                fields = fields + jnp.dot(extra[f], lane, preferred_element_type=F32)
            put(f if f < 3 else f + 1, jnp.sum(jnp.where(here, fields, 0.0), axis=0, keepdims=True))
        put(3, jnp.sum(hot, axis=0, keepdims=True))
        put(7, jnp.zeros((1, 256), F32))
        return 0

    lax.fori_loop(0, 8, gather, 0)
    per = MOVE // BLOCK
    movers = []
    for k in range(4):
        there = pl.ds(per * k, per)
        movers.append(remote(moved.at[there], landed.at[there], 1 + k, {"dom": neighbour(k)}))
        movers[-1].start()
    for copy in movers:
        copy.wait()
    for j in range(TAIL):
        own[n_groups + j] = landed[j, 0:4, :]
        pool_ref[n_groups + j] = landed[j, 0:4, :]
        vst_ref[:, (n_groups + j) * 128 : (n_groups + j) * 128 + 128] = landed[j, 4:7, :]
    tail = remote(own.at[pl.ds(n_groups, TAIL)], pool_ref.at[pl.ds(n_own + n_groups, TAIL)], 5, partner)
    tail.start()
    per = n_ghost // 4
    ghosts = []
    for k in range(4):

        def pick(i, _):
            for u in range(8):
                gbuf[per * k + 8 * i + u] = own[ghost_ref[k, 8 * i + u]]
            return 0

        lax.fori_loop(0, per // 8, pick, 0)
        there = pl.ds(2 * n_own + per * k, per)
        ghosts.append(remote(gbuf.at[pl.ds(per * k, per)], pool_ref.at[there], 6 + k, {"dom": neighbour(k)}))
        ghosts[-1].start()

    def stage(i, _):
        for u in range(16):
            lanes = pl.ds(pl.multiple_of((16 * i + u) * 128, 128), 128)
            xst_ref[:, lanes] = own[16 * i + u, 0:3, :]
        return 0

    lax.fori_loop(0, n_own // 16, stage, 0)
    for copy in (*ghosts, body, listed, tail, kept):
        copy.wait()


def features(block, row):
    pos = jnp.where(row < 3, jnp.concatenate([block, jnp.zeros_like(block)], axis=0) * ROOT, 0.0)
    return pos, jnp.sum(pos * pos, axis=0, keepdims=True), block[3:4]


def share_pairs(mine, theirs, work, n_own):
    here, there = mine[2, 0], theirs[2, 0]
    extra = jnp.abs(here - there) // 2

    def copy(i, _):
        for u in range(8):
            for side in range(2):
                work[side, 8 * i + u] = mine[side, 8 * i + u]
        return 0

    lax.fori_loop(0, (here + 7) // 8, copy, 0)

    def more(state):
        p, moved, _ = state
        return (moved < extra) & (p > 0)

    def give(state):
        p, moved, free = state
        for _ in range(8):
            at = jnp.maximum(p - 1, 0)
            a, b = work[0, at], work[1, at]
            gone = ((b < 2 * n_own) & (moved < extra)) | (p <= 0)
            keep = jnp.where(gone, work.shape[1] - 1, free - 1)
            work[0, keep] = a
            work[1, keep] = b
            moved = moved + jnp.where(gone & (p > 0), 1, 0)
            free = jnp.where(gone, free, free - 1)
            p = jnp.maximum(p - 1, 0)
        return p, moved, free

    def take(state):
        p, moved, end = state
        for _ in range(8):
            at = jnp.maximum(p - 1, 0)
            a, b = theirs[0, at], theirs[1, at]
            ours = (b < 2 * n_own) & (moved < extra) & (p > 0)
            work[0, end] = a + n_own
            work[1, end] = jnp.where(b < n_own, b + n_own, b - n_own)
            moved = moved + jnp.where(ours, 1, 0)
            end = end + jnp.where(ours, 1, 0)
            p = jnp.maximum(p - 1, 0)
        return p, moved, end

    def giver():
        p, moved, free = lax.while_loop(more, give, (here, jnp.int32(0), here))
        return here - moved, p, free - p

    def taker():
        _, _, end = lax.while_loop(more, take, (there, jnp.int32(0), here))
        return end, end, jnp.int32(0)

    return lax.cond(here > there, giver, taker)


def pair_kernel(mine, theirs, pool, xst_ref, acc_ref, npos_ref, lefts, rights, nears, highs, lows, work, sem):
    n_own = xst_ref.shape[1] // 128
    staged = pltpu.make_async_copy(xst_ref, npos_ref, sem.at[0])
    staged.start()
    acc_ref[...] = jnp.zeros_like(acc_ref)
    rights[...] = jnp.zeros_like(rights)
    count, turn_at, skip = share_pairs(mine, theirs, work, n_own)
    row = lax.broadcasted_iota(jnp.int32, (8, 128), 0)

    def cat(parts, axis):
        return jnp.concatenate(parts, axis=axis)

    def blocks_of(p):
        p = jnp.clip(p, 0, count - 1)
        p = p + jnp.where(p >= turn_at, skip, 0)
        return work[0, p], work[1, p]

    def prepare(t, slot):
        left = []
        for u in range(GROUP):
            a, b = blocks_of(t * GROUP + u)
            pa, na, wa = features(pool[a], row)
            pb, nb, wb = features(pool[b], row)
            near = jnp.where(row < 3, 2.0 * pa, jnp.where(row == 3, -1.0, jnp.where(row == 4, CUT - na, jnp.where(row == 5, wa, 0.0))))
            far = jnp.where(row < 3, pb, jnp.where(row == 3, nb, jnp.where(row == 4, 1.0, jnp.where(row == 7, wb, 0.0))))
            ah, am, al = split3(near)
            bh, bm, bl = split3(far)
            v = u % 2
            left.append(cat([ah, ah, ah, am, am, al], 0).astype(BF))
            right = cat([bh, bm, bl, bh, bm, bh], 0).astype(BF)
            rights[slot, u // 2, 48 * v : 48 * v + 48, 128 * v : 128 * v + 128] = right
            nears[slot, u] = cat([ah, am, al, bh, bm, bl], 0).astype(BF)
        for c in range(GROUP // 2):
            lefts[slot, c] = cat(left[2 * c : 2 * c + 2], 0).T

    def strengths(slot):
        for c in range(GROUP // 2):
            raw = jnp.dot(lefts[slot, c], rights[slot, c], preferred_element_type=F32)
            inv = lax.rsqrt((CUT + SOFT) - raw)
            ratio = jnp.maximum(raw, 0.0) * inv
            s = (ratio * ratio) * (inv * jnp.exp2(raw))
            high = s.astype(BF)
            highs[slot, :, 256 * c : 256 * c + 256] = high
            lows[slot, :, 256 * c : 256 * c + 256] = (s - high.astype(F32)).astype(BF)

    def sums(t, slot):
        found = []
        for u in range(GROUP):
            p = t * GROUP + u
            a, b = blocks_of(p)
            xa, xb = pool[a], pool[b]
            lanes = slice(128 * u, 128 * u + 128)
            high, low = highs[slot, :, lanes], lows[slot, :, lanes]
            f = nears[slot, u]
            both = jnp.dot(
                cat([f, f], 1),
                cat([cat([high, high.T], 1), cat([low, low.T], 1)], 0),
                preferred_element_type=F32,
            )
            g = both[0:8, :128] + both[8:16, :128] + both[16:24, :128]
            h = both[24:32, 128:] + both[32:40, 128:] + both[40:48, 128:]
            on = (p >= 0) & (p < count)
            on_far = (0.5 * g[:4] - (ROOT * xb) * g[5:6]) * (SCALE * xb[3:4])
            on_near = (h[:4] - (ROOT * xa) * h[7:8]) * (SCALE * xa[3:4])
            found.append((a, b, jnp.where(on, on_near, 0.0), jnp.where(on, on_far, 0.0)))
        for a, b, on_near, on_far in found:
            acc_ref[a] += on_near
            acc_ref[b] += on_far

    def turn(i, _):
        for v in range(3):
            t = 3 * i + v
            prepare(t, v)
            strengths((v + 2) % 3)
            sums(t - 2, (v + 1) % 3)
        return 0

    steps = (count + GROUP - 1) // GROUP + 2
    lax.fori_loop(0, (steps + 2) // 3, turn, 0)
    staged.wait()


def return_kernel(acc_ref, pret_ref, gret_ref, send, recv):
    n_own = pret_ref.shape[0]
    per = gret_ref.shape[0] // 4
    greet()
    copies = [
        pltpu.make_async_remote_copy(
            src_ref=acc_ref.at[pl.ds(n_own, n_own)],
            dst_ref=pret_ref,
            send_sem=send.at[0],
            recv_sem=recv.at[0],
            device_id={"slab": 1 - lax.axis_index("slab")},
            device_id_type=MESH,
        )
    ]
    for k in range(4):
        copies.append(
            pltpu.make_async_remote_copy(
                src_ref=acc_ref.at[pl.ds(2 * n_own + per * k, per)],
                dst_ref=gret_ref.at[pl.ds(per * k, per)],
                send_sem=send.at[1 + k],
                recv_sem=recv.at[1 + k],
                device_id={"dom": neighbour(k ^ 1)},
                device_id_type=MESH,
            )
        )
    for copy in copies:
        copy.start()
    for copy in copies:
        copy.wait()


def finish_kernel(ghost_ref, vst_ref, acc_ref, pret_ref, gret_ref, nvel_ref):
    per = ghost_ref.shape[1]

    def write(i, _):
        for u in range(16):
            b = i * 16 + u
            lanes = pl.ds(pl.multiple_of(b * 128, 128), 128)
            nvel_ref[:, lanes] = vst_ref[:, lanes] + (acc_ref[b, 0:3, :] + pret_ref[b, 0:3, :])
        return 0

    lax.fori_loop(0, pret_ref.shape[0] // 16, write, 0)

    def back(i, _):
        for k in range(4):
            for u in range(8):
                lanes = pl.ds(pl.multiple_of(ghost_ref[k, 8 * i + u] * 128, 128), 128)
                nvel_ref[:, lanes] += gret_ref[per * k + 8 * i + u, 0:3, :]
        return 0

    lax.fori_loop(0, per // 8, back, 0)


def shards(positions, velocities, destination, live_count, ghost_list, pair_blocks, pair_count):
    n_rows = positions.shape[1]
    n_groups = n_rows // BLOCK
    n_own = n_groups + TAIL
    n_ghost = 4 * ghost_list.shape[2]
    n_pool = 2 * n_own + n_ghost
    smem = pl.BlockSpec(memory_space=pltpu.SMEM)
    vmem = pl.BlockSpec(memory_space=pltpu.VMEM)
    hbm = pl.BlockSpec(memory_space=pltpu.HBM)
    ghosts = ghost_list[0]
    pairs = pair_blocks[0].T
    lists = jax.ShapeDtypeStruct((4, pairs.shape[1]), jnp.int32)

    pool, xst, vst, mine, theirs = pl.pallas_call(
        exchange_kernel,
        out_shape=(
            jax.ShapeDtypeStruct((n_pool, 4, BLOCK), F32),
            jax.ShapeDtypeStruct((3, n_own * BLOCK), F32),
            jax.ShapeDtypeStruct((3, n_own * BLOCK), F32),
            lists,
            lists,
        ),
        in_specs=[hbm, hbm, hbm, hbm, hbm, smem, smem],
        out_specs=(vmem, vmem, vmem, vmem, vmem),
        scratch_shapes=[
            pltpu.VMEM((4, n_rows), F32),
            pltpu.VMEM((4, n_rows), F32),
            pltpu.VMEM((n_groups, BLOCK), jnp.int32),
            pltpu.VMEM(pairs.shape, jnp.int32),
            pltpu.SMEM(ghosts.shape, jnp.int32),
            pltpu.VMEM((n_own, 4, BLOCK), F32),
            pltpu.VMEM((8 * n_groups, BLOCK), F32),
            pltpu.VMEM((8 * n_groups, BLOCK), F32),
            pltpu.VMEM((6, n_groups, 2 * BLOCK), BF),
            pltpu.VMEM((3, n_groups, BLOCK), BF),
            pltpu.VMEM((4, BLOCK, n_groups), BF),
            pltpu.VMEM((4, 2, n_groups, BLOCK), F32),
            pltpu.VMEM((TAIL, 8, BLOCK), F32),
            pltpu.VMEM((TAIL, 8, BLOCK), F32),
            pltpu.VMEM((n_ghost, 4, BLOCK), F32),
            pltpu.SemaphoreType.DMA((6,)),
            pltpu.SemaphoreType.DMA((11,)),
            pltpu.SemaphoreType.DMA((11,)),
        ],
        compiler_params=pltpu.CompilerParams(
            collective_id=0, has_side_effects=True, vmem_limit_bytes=32 << 20
        ),
        name="exchange",
    )(positions, velocities, destination.reshape(n_groups, BLOCK), pairs, ghosts, live_count, pair_count)

    acc, new_positions = pl.pallas_call(
        pair_kernel,
        out_shape=(
            jax.ShapeDtypeStruct((n_pool, 4, BLOCK), F32),
            jax.ShapeDtypeStruct((3, n_own * BLOCK), F32),
        ),
        in_specs=[smem, smem, vmem, vmem],
        out_specs=(vmem, hbm),
        scratch_shapes=[
            pltpu.VMEM((3, GROUP // 2, BLOCK, 96), BF),
            pltpu.VMEM((3, GROUP // 2, 96, 2 * BLOCK), BF),
            pltpu.VMEM((3, GROUP, 48, BLOCK), BF),
            pltpu.VMEM((3, BLOCK, GROUP * BLOCK), BF),
            pltpu.VMEM((3, BLOCK, GROUP * BLOCK), BF),
            pltpu.SMEM((2, 2 * pairs.shape[1]), jnp.int32),
            pltpu.SemaphoreType.DMA((1,)),
        ],
        compiler_params=pltpu.CompilerParams(vmem_limit_bytes=32 << 20),
        name="pairs",
    )(mine, theirs, pool, xst)

    pret, gret = pl.pallas_call(
        return_kernel,
        out_shape=(
            jax.ShapeDtypeStruct((n_own, 4, BLOCK), F32),
            jax.ShapeDtypeStruct((n_ghost, 4, BLOCK), F32),
        ),
        in_specs=[vmem],
        out_specs=(vmem, vmem),
        scratch_shapes=[pltpu.SemaphoreType.DMA((5,)), pltpu.SemaphoreType.DMA((5,))],
        compiler_params=pltpu.CompilerParams(
            collective_id=1, has_side_effects=True, vmem_limit_bytes=16 << 20
        ),
        name="returns",
    )(acc)

    new_velocities = pl.pallas_call(
        finish_kernel,
        out_shape=jax.ShapeDtypeStruct((3, n_own * BLOCK), F32),
        in_specs=[smem, vmem, vmem, vmem, vmem],
        out_specs=vmem,
        compiler_params=pltpu.CompilerParams(vmem_limit_bytes=32 << 20),
        name="finish",
    )(ghosts, vst, acc, pret, gret)
    return new_positions, new_velocities


def solution(mesh):
    return jax.shard_map(
        shards,
        mesh=mesh,
        in_specs=(
            P(None, ("dom", "slab")),
            P(None, ("dom", "slab")),
            P(("dom", "slab")),
            P(("dom", "slab")),
            P(("dom", "slab"), None, None),
            P(("dom", "slab"), None, None),
            P(("dom", "slab")),
        ),
        out_specs=(P(None, ("dom", "slab")), P(None, ("dom", "slab"))),
        check_vma=False,
    )
```
